32 devices in a mesh: grp: 2 (over y), chan: 4 (over x, core), tm: 4 (over z).
Axes of the slice: x: 2, y: 2, z: 4, core: 2. Of those that a mesh axis runs over, the one named last changes fastest.
Arguments:
- spectra: bfloat16 [4096, 128, 128], P(('grp', 'chan'), 'tm'), parts along dimension 0, may hold values from -6 to 6
- band_width: int32 [8], P(('grp', 'chan')), parts along dimension 0, may hold values from 512 to 1024, as said below
- pair_list: int32 [2, 32768], P(None, ('grp', 'chan')), parts along dimension 1, may hold values from 0 to 1023, as said below
- owner_ids: int32 [32768], P(('grp', 'chan')), parts along dimension 0, may hold values from 0 to 3, as said below
Outputs:
- stacks: float32 [65536, 128], P(('grp', 'chan', 'tm')), parts along dimension 0
The draws below stay inside these ranges and needn't reach their ends.
There are 2 independent parts, one for each index of `grp`. The reference program is written for one: setup_inputs(seed, part) draws one part's arguments, and reference() takes and returns one part's arrays. A program takes and returns all parts, laid end to end along the dimension named above; each array names one. Nothing has to cross between parts.
Inputs may be any that keep to these rules, and one draw needn't show every extreme that they name: `band_width`: one block has a band of exactly 1024. `pair_list`: row 0 is below 512; row 1 is below the band of the pair's block; some pair reaches its block's band minus one. `owner_ids`: among the 4096 pairs of one block no owner appears more than 2048 times, and one owner exactly 2048 times.
All inputs are finite; a program needn't handle non-finite values.
Results may differ from the reference program's by a relative error of at most 0.0003.
Values may be sent and summed in bfloat16 or wider, within the bound.
A program may use at most 128 MiB of HBM per device.

```python
import math
import jax
import jax.numpy as jnp
from jax import lax

F = 64
CH_DEV = 512
NP_DEV = 4096
K_SH = 2
BLOCKS = 4
CHANNELS = 2048
WINDOWS = 128
NPAIRS = 16384
LAGS = 128
CAP = 2048
STACK_ROWS = 32768
N_TM = 4


def band_draw(key):
    widths = jax.random.randint(jax.random.fold_in(key, 11), (BLOCKS,), CH_DEV, K_SH * CH_DEV + 1)
    widest = jax.random.randint(jax.random.fold_in(key, 12), (), 0, BLOCKS)
    return jnp.where(jnp.arange(BLOCKS) == widest, K_SH * CH_DEV, widths).astype(jnp.int32)


def draw_band_width(key, part):
    return band_draw(key)


def draw_pair_list(key, part):
    widths = band_draw(key)
    key = jax.random.fold_in(key, 3)
    sources = jax.random.randint(jax.random.fold_in(key, 1), (BLOCKS, NP_DEV), 0, CH_DEV)
    offsets = jax.random.randint(jax.random.fold_in(key, 2), (BLOCKS, NP_DEV), 0, widths[:, None])
    column = jnp.arange(NP_DEV)[None, :]
    offsets = jnp.where(column == 0, widths[:, None] - 1, offsets)
    sources = jnp.where(column == 1, 0, sources)
    return jnp.stack([sources.reshape(-1), offsets.reshape(-1)]).astype(jnp.int32)


def draw_owner_ids(key, part):
    key = jax.random.fold_in(key, 5)
    block_keys = jax.random.split(key, BLOCKS)

    def one_block(block_key):
        ordering = jax.random.permutation(jax.random.fold_in(block_key, 1), NP_DEV)
        busiest = jax.random.randint(jax.random.fold_in(block_key, 2), (), 0, N_TM)
        places = jnp.arange(NP_DEV)
        by_place = jnp.where(places < CAP, busiest, (busiest + 1 + (places - CAP) % (N_TM - 1)) % N_TM)
        return jnp.zeros((NP_DEV,), jnp.int32).at[ordering].set(by_place.astype(jnp.int32))
    return jax.vmap(one_block)(block_keys).reshape(-1).astype(jnp.int32)


def levels(stream_key, extent, cuts, least, high):
    def one(position, parts):
        steps = jax.random.uniform(jax.random.fold_in(jax.random.fold_in(stream_key, 6), position), (parts,), jnp.float32, least / len(cuts), high / len(cuts))
        return jnp.repeat(jnp.exp(steps), extent[position] // parts).reshape((-1,) + (1,) * (len(extent) - position - 1))

    gain = one(*cuts[0])
    for cut in cuts[1:]:
        gain = gain * one(*cut)
    return gain


def scatter_about(key, dims, spread, bound, shards=(), kind=jnp.bfloat16):
    values = spread * jax.random.normal(key, dims, jnp.float32)
    if shards:
        values = values * levels(key, dims, shards, -0.22, 0.18)
    return jnp.clip(values, -bound, bound).astype(kind)


def setup_inputs(seed: int = 0, part: int = 0) -> dict:
    seeds = jax.random.split(jax.random.key(seed), 5)
    own_keys = jax.random.split(jax.random.fold_in(seeds[4], part), 5)
    return {
        "spectra": scatter_about(own_keys[0], (CHANNELS, WINDOWS, 2 * F), 1.0, 6.0, ((0, 4), (1, 4))),
        "band_width": draw_band_width(jax.random.fold_in(jax.random.fold_in(seeds[4], part), 71), part),
        "pair_list": draw_pair_list(jax.random.fold_in(jax.random.fold_in(seeds[4], part), 71), part),
        "owner_ids": draw_owner_ids(jax.random.fold_in(jax.random.fold_in(seeds[4], part), 71), part),
    }


def reference(spectra, band_width, pair_list, owner_ids):
    values = spectra.astype(jnp.float32)
    block_ids = jnp.repeat(jnp.arange(BLOCKS, dtype=jnp.int32), NP_DEV)
    sources = block_ids * CH_DEV + pair_list[0]
    receivers = (sources + pair_list[1]) % CHANNELS
    group_size = math.gcd(NPAIRS, 256)

    def cross_block(indices):
        source_ids, receiver_ids = indices
        source_rows = values[source_ids]
        receiver_rows = values[receiver_ids]
        source_re = source_rows[..., :F]
        source_im = source_rows[..., F:]
        receiver_re = receiver_rows[..., :F]
        receiver_im = receiver_rows[..., F:]
        real_part = jnp.einsum("pwf,pwf->pf", source_re, receiver_re) + jnp.einsum("pwf,pwf->pf", source_im, receiver_im)
        imag_part = jnp.einsum("pwf,pwf->pf", source_im, receiver_re) - jnp.einsum("pwf,pwf->pf", source_re, receiver_im)
        return real_part, imag_part

    real_part, imag_part = lax.map(cross_block, (sources.reshape(-1, group_size), receivers.reshape(-1, group_size)))
    real_part = real_part.reshape(NPAIRS, F) / WINDOWS
    imag_part = imag_part.reshape(NPAIRS, F) / WINDOWS
    spectrum = real_part + 1j * imag_part
    padded = jnp.concatenate([spectrum, jnp.zeros((NPAIRS, 1), spectrum.dtype)], axis=1)
    correlation = (jnp.fft.irfft(padded, n=LAGS, axis=1) * LAGS).astype(jnp.float32)
    tapering = 1.0 - pair_list[1].astype(jnp.float32) / band_width[block_ids].astype(jnp.float32)
    weighted = correlation * tapering[:, None]
    owners = owner_ids.reshape(BLOCKS, NP_DEV)
    onehot = (owners[:, :, None] == jnp.arange(N_TM, dtype=jnp.int32)[None, None, :]).astype(jnp.int32)
    ranking = (jnp.cumsum(onehot, axis=1) - 1).astype(jnp.int32)
    slot_ids = jnp.sum(ranking * onehot, axis=2).astype(jnp.int32).reshape(-1)
    targets = ((block_ids * N_TM + owner_ids) * CAP + slot_ids).astype(jnp.int32)
    return jnp.zeros((STACK_ROWS, LAGS), jnp.float32).at[targets].set(weighted)
```

```python
import math

import jax
import jax.numpy as jnp
import numpy as np
from jax import lax
from jax.experimental import pallas as pl
from jax.experimental.pallas import tpu as pltpu
from jax.sharding import PartitionSpec as P

K_SH = 2
GROUP = 16


def from_behind(block, axis, distance):
    devices = range(lax.axis_size(axis))
    route = [((i - distance) % len(devices), i) for i in devices]
    return lax.ppermute(block, axis, route)


def inverse_table(half_bins):
    length = 2 * half_bins
    row_ids = np.arange(length)
    frequency = row_ids % half_bins
    phases = (frequency[:, None] * np.arange(length)[None, :] % length) * (2.0 * math.pi / length)
    weights = np.where(frequency == 0, 1.0, 2.0)[:, None]
    return np.where(
        (row_ids >= half_bins)[:, None], -weights * np.sin(phases), weights * np.cos(phases)
    ).astype(np.float32)


def gather_rows(parts):
    row = lax.broadcasted_iota(jnp.int32, parts[0].shape, 0)
    span = 4
    while span:
        keep = (row // span) % 2 == 0
        half = len(parts) // 2
        parts = [
            jnp.where(keep, parts[k], pltpu.roll(parts[k + half], span, 0))
            + jnp.where(keep, pltpu.roll(parts[k], 8 - span, 0), parts[k + half])
            for k in range(half)
        ]
        span //= 2
    return parts[0]


def sum_tiles(rows):
    total = rows[0:8]
    for start in range(8, rows.shape[0], 8):
        total = total + rows[start : start + 8]
    return total


def cross_rows(sources, receivers, near, turned, total, add):
    npairs = total.shape[0]
    half = total.shape[1] // 2

    def step(group, carry):
        first = pl.multiple_of(group * GROUP, GROUP)
        for offset in range(0, GROUP, 8):
            same, crossed = [], []
            for k in range(8):
                pair = first + offset + k
                source = sources[pair]
                receiver_row = near[receivers[pair]].astype(jnp.float32)
                same.append(sum_tiles(near[source].astype(jnp.float32) * receiver_row))
                crossed.append(sum_tiles(turned[source].astype(jnp.float32) * receiver_row))
            same = gather_rows(same)
            crossed = gather_rows(crossed)
            lane = lax.broadcasted_iota(jnp.int32, same.shape, 1)
            rows = jnp.where(
                lane < half,
                same + pltpu.roll(same, half, 1),
                pltpu.roll(crossed, half, 1) - crossed,
            )
            place = pl.ds(pl.multiple_of(first + offset, 8), 8)
            if add:
                rows = rows + total[place, :]
            total[place, :] = rows
        return carry

    lax.fori_loop(0, npairs // GROUP, step, 0)


def turn_rows(near, turned):
    half = turned.shape[2] // 2

    def step(channel, carry):
        turned[channel] = pltpu.roll(near[channel].astype(jnp.float32), half, 1).astype(
            jnp.bfloat16
        )
        return carry

    lax.fori_loop(0, turned.shape[0], step, 0, unroll=8)


def cross_kernel(sources, receivers, own, ahead, second, total, near, turned, sems):
    rows = own.shape[0]
    copies = [
        pltpu.make_async_copy(block, near.at[pl.ds(k * rows, rows)], sems.at[k])
        for k, block in enumerate((own, ahead, second))
    ]
    for copy in copies:
        copy.start()
    copies[0].wait()
    turn_rows(near, turned)
    for copy in copies[1:]:
        copy.wait()
    cross_rows(sources, receivers, near, turned, total, False)


def stack_kernel(owners, tapering, sums, table, out, rows):
    me = lax.axis_index("tm")
    npairs = sums.shape[0]
    capacity, length = out.shape
    rows[...] = jnp.zeros_like(rows)

    def step(group, count):
        for k in range(8):
            pair = group * 8 + k
            rows[pl.ds(count, 1), :] = sums[pl.ds(pair, 1), :] * tapering[pair]
            count = count + (owners[pair] == me).astype(jnp.int32)
        return count

    count = lax.fori_loop(0, npairs // 8, step, jnp.int32(0))
    rows[pl.ds(count, 1), :] = jnp.zeros((1, length), jnp.float32)
    out[...] = jnp.dot(
        rows[0:capacity, :],
        table[...],
        precision=lax.Precision.HIGHEST,
        preferred_element_type=jnp.float32,
    )


def shards(spectra, band_width, pair_list, owner_ids):
    channel_rows, window_rows, length = spectra.shape
    npairs = pair_list.shape[1]
    tm_size = lax.axis_size("tm")
    capacity = 2 * npairs // tm_size
    windows = window_rows * tm_size
    ahead = from_behind(spectra, "chan", -1)
    second = from_behind(spectra, "chan", -2)
    sources = pair_list[0]
    offsets = pair_list[1]
    receivers = sources + offsets
    smem = pl.BlockSpec(memory_space=pltpu.SMEM)
    vmem = pl.BlockSpec(memory_space=pltpu.VMEM)
    hbm = pl.BlockSpec(memory_space=pl.ANY)
    total = pl.pallas_call(
        cross_kernel,
        out_shape=jax.ShapeDtypeStruct((npairs, length), jnp.float32),
        in_specs=[smem, smem, hbm, hbm, hbm],
        out_specs=vmem,
        scratch_shapes=[
            pltpu.VMEM(((K_SH + 1) * channel_rows, window_rows, length), jnp.bfloat16),
            pltpu.VMEM((channel_rows, window_rows, length), jnp.bfloat16),
            pltpu.SemaphoreType.DMA((3,)),
        ],
        compiler_params=pltpu.CompilerParams(vmem_limit_bytes=40 * 2**20),
        cost_estimate=pl.CostEstimate(
            flops=8 * npairs * window_rows * length, bytes_accessed=14 * 2**20, transcendentals=0
        ),
    )(sources, receivers, spectra, ahead, second)
    total = lax.psum(total, "tm")
    tapering = (1.0 - offsets.astype(jnp.float32) / band_width[0].astype(jnp.float32)) / windows
    return pl.pallas_call(
        stack_kernel,
        out_shape=jax.ShapeDtypeStruct((capacity, length), jnp.float32),
        in_specs=[smem, smem, vmem, vmem],
        out_specs=vmem,
        scratch_shapes=[pltpu.VMEM((capacity + 8, length), jnp.float32)],
        compiler_params=pltpu.CompilerParams(vmem_limit_bytes=32 * 2**20),
        cost_estimate=pl.CostEstimate(
            flops=12 * capacity * length * length, bytes_accessed=3 * 2**20, transcendentals=0
        ),
    )(owner_ids, tapering, total, jnp.asarray(inverse_table(length // 2)))


def solution(mesh):
    return jax.shard_map(
        shards,
        mesh=mesh,
        in_specs=(
            P(("grp", "chan"), "tm", None),
            P(("grp", "chan")),
            P(None, ("grp", "chan")),
            P(("grp", "chan")),
        ),
        out_specs=P(("grp", "chan", "tm"), None),
        check_vma=False,
    )
```

```python
import functools
import math

import jax
import jax.numpy as jnp
import numpy as np
from jax import lax
from jax.experimental import pallas as pl
from jax.experimental.pallas import tpu as pltpu
from jax.sharding import PartitionSpec as P

K_SH = 2
GROUP = 16
CHUNK = 16
PIECES = 4
DEPTH = 3
FLOWS = 16
MESH = pl.DeviceIdType.MESH


def inverse_table(half_bins):
    length = 2 * half_bins
    row_ids = np.arange(length)
    frequency = row_ids % half_bins
    phases = (frequency[:, None] * np.arange(length)[None, :] % length) * (2.0 * math.pi / length)
    weights = np.where(frequency == 0, 1.0, 2.0)[:, None]
    return np.where(
        (row_ids >= half_bins)[:, None], -weights * np.sin(phases), weights * np.cos(phases)
    ).astype(np.float32)


def gather_rows(parts):
    row = lax.broadcasted_iota(jnp.int32, parts[0].shape, 0)
    span = 4
    while span:
        keep = (row // span) % 2 == 0
        half = len(parts) // 2
        parts = [
            jnp.where(keep, parts[k], pltpu.roll(parts[k + half], span, 0))
            + jnp.where(keep, pltpu.roll(parts[k], 8 - span, 0), parts[k + half])
            for k in range(half)
        ]
        span //= 2
    return parts[0]


def sum_tiles(rows):
    total = rows[0:8]
    for start in range(8, rows.shape[0], 8):
        total = total + rows[start : start + 8]
    return total


def cross_rows(sources, receivers, near, turned, total, start, count, add):
    half = total.shape[1] // 2

    def step(group, carry):
        first = pl.multiple_of(start + group * GROUP, GROUP)
        for offset in range(0, GROUP, 8):
            same, crossed = [], []
            for k in range(8):
                pair = first + offset + k
                source = sources[pair]
                receiver_row = near[receivers[pair]].astype(jnp.float32)
                same.append(sum_tiles(near[source].astype(jnp.float32) * receiver_row))
                crossed.append(sum_tiles(turned[source].astype(jnp.float32) * receiver_row))
            same = gather_rows(same)
            crossed = gather_rows(crossed)
            lane = lax.broadcasted_iota(jnp.int32, same.shape, 1)
            rows = jnp.where(
                lane < half,
                same + pltpu.roll(same, half, 1),
                pltpu.roll(crossed, half, 1) - crossed,
            )
            place = pl.ds(pl.multiple_of(first + offset, 8), 8)
            if add:
                rows = rows + total[place, :]
            total[place, :] = rows
        return carry

    lax.fori_loop(0, count // GROUP, step, 0)


def turn_rows(near, turned):
    half = turned.shape[2] // 2

    def step(channel, carry):
        turned[channel] = pltpu.roll(near[channel].astype(jnp.float32), half, 1).astype(
            jnp.bfloat16
        )
        return carry

    lax.fori_loop(0, turned.shape[0], step, 0, unroll=8)


def exchange_kernel(
    nchan, ntm, sources, receivers, own, total, *scratch
):
    chunks = own.shape[1] // CHUNK
    near = scratch[:chunks]
    (
        turned, mine, from_left, to_right, from_right, to_left,
        own_sems, far_send, far_recv, pass_send, pass_recv,
        right_send, right_recv, left_send, left_recv,
    ) = scratch[chunks:]
    rows = own.shape[0]
    piece_rows = rows // PIECES
    chan = lax.axis_index("chan")
    me = lax.axis_index("tm")
    core = lax.rem(chan, 2)
    partner = chan + 1 - 2 * core
    behind = lax.rem(chan + nchan - 2, nchan)
    beyond = lax.rem(chan + 2, nchan)
    last = ntm - 1

    barrier = pltpu.get_barrier_semaphore()
    peers = (behind, partner) if nchan == 4 else (behind, beyond, partner)
    for device in peers:
        pl.semaphore_signal(barrier, inc=1, device_id={"chan": device}, device_id_type=MESH)

    @pl.when(me > 0)
    def _():
        pl.semaphore_signal(barrier, inc=1, device_id={"tm": me - 1}, device_id_type=MESH)

    @pl.when(me < last)
    def _():
        pl.semaphore_signal(barrier, inc=1, device_id={"tm": me + 1}, device_id_type=MESH)

    own_copies = []
    for chunk in range(chunks):
        copy = pltpu.make_async_copy(
            own.at[:, pl.ds(chunk * CHUNK, CHUNK), :],
            near[chunk].at[pl.ds(0, rows)],
            own_sems.at[chunk],
        )
        own_copies.append(copy)
    own_copies[0].start()

    pl.semaphore_wait(
        barrier, len(peers) + (me > 0).astype(jnp.int32) + (me < last).astype(jnp.int32)
    )

    def own_piece(number):
        chunk, piece = divmod(number, PIECES)
        return own.at[pl.ds(piece * piece_rows, piece_rows), pl.ds(chunk * CHUNK, CHUNK), :]

    def near_piece(number, block):
        chunk, piece = divmod(number, PIECES)
        return near[chunk].at[pl.ds(block * rows + piece * piece_rows, piece_rows)]

    def far(number):
        return pltpu.make_async_remote_copy(
            src_ref=own_piece(number),
            dst_ref=near_piece(number, 2),
            send_sem=far_send.at[number],
            recv_sem=far_recv.at[number],
            device_id={"chan": behind},
            device_id_type=MESH,
        )

    def handed(number, source):
        return pltpu.make_async_remote_copy(
            src_ref=source,
            dst_ref=near_piece(number, 1),
            send_sem=pass_send.at[number],
            recv_sem=pass_recv.at[number],
            device_id={"chan": partner},
            device_id_type=MESH,
        )

    count = chunks * PIECES
    for number in range(min(DEPTH, count)):
        far(number).start()

    for copy in own_copies[1:]:
        copy.start()

    @pl.when(core == 1)
    def _():
        for number in range(count):
            handed(number, own_piece(number)).start()

    def arrive(number):
        far(number).wait_recv()
        if number + DEPTH < count:
            far(number + DEPTH).start()

        @pl.when(core == 0)
        def _():
            handed(number, near_piece(number, 2)).start()

    group_rows = mine.shape[0] // FLOWS
    for chunk in range(chunks):
        own_copies[chunk].wait()
        turn_rows(near[chunk], turned)
        for piece in range(PIECES):
            arrive(chunk * PIECES + piece)
        for piece in range(PIECES):
            handed(chunk * PIECES + piece, own_piece(chunk * PIECES + piece)).wait_recv()
        if chunk < chunks - 1:
            cross_rows(
                sources, receivers, near[chunk], turned, mine, 0, mine.shape[0], chunk > 0
            )

    def flow(source, target, send_sem, recv_sem, group, device):
        place = pl.ds(pl.multiple_of(group * group_rows, group_rows), group_rows)
        return pltpu.make_async_remote_copy(
            src_ref=source.at[place],
            dst_ref=target.at[place],
            send_sem=send_sem.at[group],
            recv_sem=recv_sem.at[group],
            device_id={"tm": device},
            device_id_type=MESH,
        )

    def rightward(group):
        return flow(to_right, from_left, right_send, right_recv, group, lax.rem(me + 1, ntm))

    def leftward(group):
        return flow(to_left, from_right, left_send, left_recv, group, lax.rem(me + last, ntm))

    def place_of(group):
        return pl.ds(pl.multiple_of(group * group_rows, group_rows), group_rows)

    def stage(step, carry):
        @pl.when(step < FLOWS)
        def _():
            cross_rows(
                sources, receivers, near[chunks - 1], turned, mine,
                step * group_rows, group_rows, chunks > 1,
            )

        right_group = step - me

        @pl.when((right_group >= 0) & (right_group < FLOWS) & (me < last))
        def _():
            place = place_of(right_group)

            @pl.when(me > 0)
            def _():
                rightward(right_group).wait_recv()
                to_right[place, :] = mine[place, :] + from_left[place, :]

            @pl.when(me == 0)
            def _():
                to_right[place, :] = mine[place, :]

            rightward(right_group).start()

        left_group = step - (last - me)

        @pl.when((left_group >= 0) & (left_group < FLOWS) & (me > 0))
        def _():
            place = place_of(left_group)

            @pl.when(me < last)
            def _():
                leftward(left_group).wait_recv()
                to_left[place, :] = mine[place, :] + from_right[place, :]

            @pl.when(me == last)
            def _():
                to_left[place, :] = mine[place, :]

            leftward(left_group).start()

        return carry

    lax.fori_loop(0, FLOWS + ntm - 1, stage, 0)

    def finish(group, carry):
        place = place_of(group)

        @pl.when(me == 0)
        def _():
            leftward(group).wait_recv()
            total[place, :] = mine[place, :] + from_right[place, :]

        @pl.when(me == last)
        def _():
            rightward(group).wait_recv()
            total[place, :] = mine[place, :] + from_left[place, :]

        @pl.when((me > 0) & (me < last))
        def _():
            total[place, :] = to_right[place, :] + from_right[place, :]

        @pl.when(me < last)
        def _():
            rightward(group).wait_send()

        @pl.when(me > 0)
        def _():
            leftward(group).wait_send()

        return carry

    lax.fori_loop(0, FLOWS, finish, 0)
    for number in range(count):
        far(number).wait_send()
        handed(number, own_piece(number)).wait_send()


def stack_kernel(owners, tapering, sums, table, out, rows):
    me = lax.axis_index("tm")
    npairs = sums.shape[0]
    capacity, length = out.shape
    rows[...] = jnp.zeros_like(rows)

    def step(group, count):
        for k in range(8):
            pair = group * 8 + k
            rows[pl.ds(count, 1), :] = sums[pl.ds(pair, 1), :] * tapering[pair]
            count = count + (owners[pair] == me).astype(jnp.int32)
        return count

    count = lax.fori_loop(0, npairs // 8, step, jnp.int32(0))
    rows[pl.ds(count, 1), :] = jnp.zeros((1, length), jnp.float32)
    out[...] = jnp.dot(
        rows[0:capacity, :],
        table[...],
        precision=lax.Precision.HIGHEST,
        preferred_element_type=jnp.float32,
    )


def shards(spectra, band_width, pair_list, owner_ids):
    channel_rows, window_rows, length = spectra.shape
    npairs = pair_list.shape[1]
    tm_size = lax.axis_size("tm")
    capacity = 2 * npairs // tm_size
    windows = window_rows * tm_size
    sources = pair_list[0]
    offsets = pair_list[1]
    receivers = sources + offsets
    smem = pl.BlockSpec(memory_space=pltpu.SMEM)
    vmem = pl.BlockSpec(memory_space=pltpu.VMEM)
    hbm = pl.BlockSpec(memory_space=pl.ANY)
    chunks = window_rows // CHUNK
    flow_buffer = pltpu.VMEM((npairs, length), jnp.float32)
    total = pl.pallas_call(
        functools.partial(exchange_kernel, lax.axis_size("chan"), tm_size),
        out_shape=jax.ShapeDtypeStruct((npairs, length), jnp.float32),
        in_specs=[smem, smem, hbm],
        out_specs=vmem,
        scratch_shapes=[pltpu.VMEM(((K_SH + 1) * channel_rows, CHUNK, length), jnp.bfloat16)] * chunks
        + [pltpu.VMEM((channel_rows, CHUNK, length), jnp.bfloat16)]
        + [flow_buffer] * 5
        + [pltpu.SemaphoreType.DMA((chunks,))]
        + [pltpu.SemaphoreType.DMA((chunks * PIECES,))] * 4
        + [pltpu.SemaphoreType.DMA((FLOWS,))] * 4,
        compiler_params=pltpu.CompilerParams(
            vmem_limit_bytes=48 * 2**20, collective_id=0, has_side_effects=True
        ),
        cost_estimate=pl.CostEstimate(
            flops=8 * npairs * window_rows * length, bytes_accessed=14 * 2**20, transcendentals=0
        ),
    )(sources, receivers, spectra)
    tapering = (1.0 - offsets.astype(jnp.float32) / band_width[0].astype(jnp.float32)) / windows
    return pl.pallas_call(
        stack_kernel,
        out_shape=jax.ShapeDtypeStruct((capacity, length), jnp.float32),
        in_specs=[smem, smem, vmem, vmem],
        out_specs=vmem,
        scratch_shapes=[pltpu.VMEM((capacity + 8, length), jnp.float32)],
        compiler_params=pltpu.CompilerParams(vmem_limit_bytes=32 * 2**20),
        cost_estimate=pl.CostEstimate(
            flops=12 * capacity * length * length, bytes_accessed=3 * 2**20, transcendentals=0
        ),
    )(owner_ids, tapering, total, jnp.asarray(inverse_table(length // 2)))


def solution(mesh):
    return jax.shard_map(
        shards,
        mesh=mesh,
        in_specs=(
            P(("grp", "chan"), "tm", None),
            P(("grp", "chan")),
            P(None, ("grp", "chan")),
            P(("grp", "chan")),
        ),
        out_specs=P(("grp", "chan", "tm"), None),
        check_vma=False,
    )
```

```python
import functools
import math

import jax
import jax.numpy as jnp
import numpy as np
from jax import lax
from jax.experimental import pallas as pl
from jax.experimental.pallas import tpu as pltpu
from jax.sharding import PartitionSpec as P

K_SH = 2
GROUP = 16
CHUNK = 16
PIECES = 4
DEPTH = 4
FLOWS = 32
LAG = 2
MESH = pl.DeviceIdType.MESH


def inverse_table(half_bins):
    length = 2 * half_bins
    row_ids = np.arange(length)
    frequency = row_ids % half_bins
    phases = (frequency[:, None] * np.arange(length)[None, :] % length) * (2.0 * math.pi / length)
    weights = np.where(frequency == 0, 1.0, 2.0)[:, None]
    return np.where(
        (row_ids >= half_bins)[:, None], -weights * np.sin(phases), weights * np.cos(phases)
    ).astype(np.float32)


def gather_rows(parts):
    row = lax.broadcasted_iota(jnp.int32, parts[0].shape, 0)
    span = 4
    while span:
        keep = (row // span) % 2 == 0
        half = len(parts) // 2
        parts = [
            jnp.where(keep, parts[k], pltpu.roll(parts[k + half], span, 0))
            + jnp.where(keep, pltpu.roll(parts[k], 8 - span, 0), parts[k + half])
            for k in range(half)
        ]
        span //= 2
    return parts[0]


def sum_tiles(rows):
    total = rows[0:8]
    for start in range(8, rows.shape[0], 8):
        total = total + rows[start : start + 8]
    return total


def cross_rows(sources, receivers, near, turned, total, start, count, add):
    half = total.shape[1] // 2

    def step(group, carry):
        first = pl.multiple_of(start + group * GROUP, GROUP)
        for offset in range(0, GROUP, 8):
            same, crossed = [], []
            for k in range(8):
                pair = first + offset + k
                source = sources[pair]
                receiver_row = near[receivers[pair]].astype(jnp.float32)
                same.append(sum_tiles(near[source].astype(jnp.float32) * receiver_row))
                crossed.append(sum_tiles(turned[source].astype(jnp.float32) * receiver_row))
            same = gather_rows(same)
            crossed = gather_rows(crossed)
            lane = lax.broadcasted_iota(jnp.int32, same.shape, 1)
            rows = jnp.where(
                lane < half,
                same + pltpu.roll(same, half, 1),
                pltpu.roll(crossed, half, 1) - crossed,
            )
            place = pl.ds(pl.multiple_of(first + offset, 8), 8)
            if add:
                rows = rows + total[place, :]
            total[place, :] = rows
        return carry

    lax.fori_loop(0, count // GROUP, step, 0)


def turn_rows(near, turned):
    half = turned.shape[2] // 2

    def step(channel, carry):
        turned[channel] = pltpu.roll(near[channel].astype(jnp.float32), half, 1).astype(
            jnp.bfloat16
        )
        return carry

    lax.fori_loop(0, turned.shape[0], step, 0, unroll=8)


def exchange_kernel(
    nchan, ntm, sources, receivers, own, total, *scratch
):
    chunks = own.shape[1] // CHUNK
    near = scratch[:chunks]
    (
        turned, mine, from_left, to_right, from_right, to_left,
        own_sems, far_send, far_recv, pass_send, pass_recv,
        right_send, right_recv, left_send, left_recv,
    ) = scratch[chunks:]
    rows = own.shape[0]
    piece_rows = rows // PIECES
    chan = lax.axis_index("chan")
    me = lax.axis_index("tm")
    core = lax.rem(chan, 2)
    partner = chan + 1 - 2 * core
    behind = lax.rem(chan + nchan - 2, nchan)
    beyond = lax.rem(chan + 2, nchan)
    last = ntm - 1

    barrier = pltpu.get_barrier_semaphore()
    peers = (behind, partner) if nchan == 4 else (behind, beyond, partner)
    for device in peers:
        pl.semaphore_signal(barrier, inc=1, device_id={"chan": device}, device_id_type=MESH)

    @pl.when(me > 0)
    def _():
        pl.semaphore_signal(barrier, inc=1, device_id={"tm": me - 1}, device_id_type=MESH)

    @pl.when(me < last)
    def _():
        pl.semaphore_signal(barrier, inc=1, device_id={"tm": me + 1}, device_id_type=MESH)

    own_copies = []
    for chunk in range(chunks):
        copy = pltpu.make_async_copy(
            own.at[:, pl.ds(chunk * CHUNK, CHUNK), :],
            near[chunk].at[pl.ds(0, rows)],
            own_sems.at[chunk],
        )
        own_copies.append(copy)
    own_copies[0].start()

    pl.semaphore_wait(
        barrier, len(peers) + (me > 0).astype(jnp.int32) + (me < last).astype(jnp.int32)
    )

    def own_piece(number):
        chunk, piece = divmod(number, PIECES)
        return own.at[pl.ds(piece * piece_rows, piece_rows), pl.ds(chunk * CHUNK, CHUNK), :]

    def near_piece(number, block):
        chunk, piece = divmod(number, PIECES)
        return near[chunk].at[pl.ds(block * rows + piece * piece_rows, piece_rows)]

    def far(number):
        return pltpu.make_async_remote_copy(
            src_ref=own_piece(number),
            dst_ref=near_piece(number, 2),
            send_sem=far_send.at[number],
            recv_sem=far_recv.at[number],
            device_id={"chan": behind},
            device_id_type=MESH,
        )

    def handed(number, source):
        return pltpu.make_async_remote_copy(
            src_ref=source,
            dst_ref=near_piece(number, 1),
            send_sem=pass_send.at[number],
            recv_sem=pass_recv.at[number],
            device_id={"chan": partner},
            device_id_type=MESH,
        )

    count = chunks * PIECES
    for number in range(min(DEPTH, count)):
        far(number).start()

    for copy in own_copies[1:]:
        copy.start()

    @pl.when(core == 1)
    def _():
        for number in range(count):
            handed(number, own_piece(number)).start()

    def arrive(number):
        far(number).wait_recv()
        if number + DEPTH < count:
            far(number + DEPTH).start()

        @pl.when(core == 0)
        def _():
            handed(number, near_piece(number, 2)).start()

    group_rows = mine.shape[0] // FLOWS
    for chunk in range(chunks):
        own_copies[chunk].wait()
        turn_rows(near[chunk], turned)
        for piece in range(PIECES):
            arrive(chunk * PIECES + piece)
        for piece in range(PIECES):
            handed(chunk * PIECES + piece, own_piece(chunk * PIECES + piece)).wait_recv()
        if chunk < chunks - 1:
            cross_rows(
                sources, receivers, near[chunk], turned, mine, 0, mine.shape[0], chunk > 0
            )

    def flow(source, target, send_sem, recv_sem, group, device):
        place = pl.ds(pl.multiple_of(group * group_rows, group_rows), group_rows)
        return pltpu.make_async_remote_copy(
            src_ref=source.at[place],
            dst_ref=target.at[place],
            send_sem=send_sem.at[group],
            recv_sem=recv_sem.at[group],
            device_id={"tm": device},
            device_id_type=MESH,
        )

    def rightward(group):
        return flow(to_right, from_left, right_send, right_recv, group, lax.rem(me + 1, ntm))

    def leftward(group):
        return flow(to_left, from_right, left_send, left_recv, group, lax.rem(me + last, ntm))

    def place_of(group):
        return pl.ds(pl.multiple_of(group * group_rows, group_rows), group_rows)

    def stage(step, carry):
        @pl.when(step < FLOWS)
        def _():
            cross_rows(
                sources, receivers, near[chunks - 1], turned, mine,
                step * group_rows, group_rows, chunks > 1,
            )

        right_group = step - LAG * me

        @pl.when((right_group >= 0) & (right_group < FLOWS) & (me < last))
        def _():
            place = place_of(right_group)

            @pl.when(me > 0)
            def _():
                rightward(right_group).wait_recv()
                to_right[place, :] = mine[place, :] + from_left[place, :]

            @pl.when(me == 0)
            def _():
                to_right[place, :] = mine[place, :]

            rightward(right_group).start()

        left_group = step - LAG * (last - me)

        @pl.when((left_group >= 0) & (left_group < FLOWS) & (me > 0))
        def _():
            place = place_of(left_group)

            @pl.when(me < last)
            def _():
                leftward(left_group).wait_recv()
                to_left[place, :] = mine[place, :] + from_right[place, :]

            @pl.when(me == last)
            def _():
                to_left[place, :] = mine[place, :]

            leftward(left_group).start()

        return carry

    lax.fori_loop(0, FLOWS + LAG * last, stage, 0)

    def finish(group, carry):
        place = place_of(group)

        @pl.when(me == 0)
        def _():
            leftward(group).wait_recv()
            total[place, :] = mine[place, :] + from_right[place, :]

        @pl.when(me == last)
        def _():
            rightward(group).wait_recv()
            total[place, :] = mine[place, :] + from_left[place, :]

        @pl.when((me > 0) & (me < last))
        def _():
            total[place, :] = to_right[place, :] + from_right[place, :]

        @pl.when(me < last)
        def _():
            rightward(group).wait_send()

        @pl.when(me > 0)
        def _():
            leftward(group).wait_send()

        return carry

    lax.fori_loop(0, FLOWS, finish, 0)
    for number in range(count):
        far(number).wait_send()
        handed(number, own_piece(number)).wait_send()


def stack_kernel(owners, tapering, sums, table, out, rows):
    me = lax.axis_index("tm")
    npairs = sums.shape[0]
    capacity, length = out.shape
    rows[...] = jnp.zeros_like(rows)

    def step(group, count):
        for k in range(32):
            pair = group * 32 + k
            rows[pl.ds(count, 1), :] = sums[pl.ds(pair, 1), :] * tapering[pair]
            count = count + (owners[pair] == me).astype(jnp.int32)
        return count

    count = lax.fori_loop(0, npairs // 32, step, jnp.int32(0))
    rows[pl.ds(count, 1), :] = jnp.zeros((1, length), jnp.float32)
    out[...] = jnp.dot(
        rows[0:capacity, :],
        table[...],
        precision=lax.Precision.HIGHEST,
        preferred_element_type=jnp.float32,
    )


def shards(spectra, band_width, pair_list, owner_ids):
    channel_rows, window_rows, length = spectra.shape
    npairs = pair_list.shape[1]
    tm_size = lax.axis_size("tm")
    capacity = 2 * npairs // tm_size
    windows = window_rows * tm_size
    sources = pair_list[0]
    offsets = pair_list[1]
    receivers = sources + offsets
    smem = pl.BlockSpec(memory_space=pltpu.SMEM)
    vmem = pl.BlockSpec(memory_space=pltpu.VMEM)
    hbm = pl.BlockSpec(memory_space=pl.ANY)
    chunks = window_rows // CHUNK
    flow_buffer = pltpu.VMEM((npairs, length), jnp.float32)
    total = pl.pallas_call(
        functools.partial(exchange_kernel, lax.axis_size("chan"), tm_size),
        out_shape=jax.ShapeDtypeStruct((npairs, length), jnp.float32),
        in_specs=[smem, smem, hbm],
        out_specs=vmem,
        scratch_shapes=[pltpu.VMEM(((K_SH + 1) * channel_rows, CHUNK, length), jnp.bfloat16)] * chunks
        + [pltpu.VMEM((channel_rows, CHUNK, length), jnp.bfloat16)]
        + [flow_buffer] * 5
        + [pltpu.SemaphoreType.DMA((chunks,))]
        + [pltpu.SemaphoreType.DMA((chunks * PIECES,))] * 4
        + [pltpu.SemaphoreType.DMA((FLOWS,))] * 4,
        compiler_params=pltpu.CompilerParams(
            vmem_limit_bytes=48 * 2**20, collective_id=0, has_side_effects=True
        ),
        cost_estimate=pl.CostEstimate(
            flops=8 * npairs * window_rows * length, bytes_accessed=14 * 2**20, transcendentals=0
        ),
    )(sources, receivers, spectra)
    tapering = (1.0 - offsets.astype(jnp.float32) / band_width[0].astype(jnp.float32)) / windows
    return pl.pallas_call(
        stack_kernel,
        out_shape=jax.ShapeDtypeStruct((capacity, length), jnp.float32),
        in_specs=[smem, smem, vmem, vmem],
        out_specs=vmem,
        scratch_shapes=[pltpu.VMEM((capacity + 8, length), jnp.float32)],
        compiler_params=pltpu.CompilerParams(vmem_limit_bytes=32 * 2**20),
        cost_estimate=pl.CostEstimate(
            flops=12 * capacity * length * length, bytes_accessed=3 * 2**20, transcendentals=0
        ),
    )(owner_ids, tapering, total, jnp.asarray(inverse_table(length // 2)))


def solution(mesh):
    return jax.shard_map(
        shards,
        mesh=mesh,
        in_specs=(
            P(("grp", "chan"), "tm", None),
            P(("grp", "chan")),
            P(None, ("grp", "chan")),
            P(("grp", "chan")),
        ),
        out_specs=P(("grp", "chan", "tm"), None),
        check_vma=False,
    )
```

```python
import functools
import math

import jax
import jax.numpy as jnp
import numpy as np
from jax import lax
from jax.experimental import pallas as pl
from jax.experimental.pallas import tpu as pltpu
from jax.sharding import PartitionSpec as P

K_SH = 2
GROUP = 16
CHUNK = 16
PIECES = 8
DEPTH = 8
FLOWS = 32
LAG = 2
MESH = pl.DeviceIdType.MESH


def inverse_table(half_bins):
    length = 2 * half_bins
    row_ids = np.arange(length)
    frequency = row_ids % half_bins
    phases = (frequency[:, None] * np.arange(length)[None, :] % length) * (2.0 * math.pi / length)
    weights = np.where(frequency == 0, 1.0, 2.0)[:, None]
    return np.where(
        (row_ids >= half_bins)[:, None], -weights * np.sin(phases), weights * np.cos(phases)
    ).astype(np.float32)


def gather_rows(parts):
    row = lax.broadcasted_iota(jnp.int32, parts[0].shape, 0)
    span = 4
    while span:
        keep = (row // span) % 2 == 0
        half = len(parts) // 2
        parts = [
            jnp.where(keep, parts[k], pltpu.roll(parts[k + half], span, 0))
            + jnp.where(keep, pltpu.roll(parts[k], 8 - span, 0), parts[k + half])
            for k in range(half)
        ]
        span //= 2
    return parts[0]


def sum_tiles(rows):
    total = rows[0:8]
    for start in range(8, rows.shape[0], 8):
        total = total + rows[start : start + 8]
    return total


def cross_rows(sources, receivers, near, turned, total, start, count, add):
    half = total.shape[1] // 2

    def step(group, carry):
        first = pl.multiple_of(start + group * GROUP, GROUP)
        for offset in range(0, GROUP, 8):
            same, crossed = [], []
            for k in range(8):
                pair = first + offset + k
                source = sources[pair]
                receiver_row = near[receivers[pair]].astype(jnp.float32)
                same.append(sum_tiles(near[source].astype(jnp.float32) * receiver_row))
                crossed.append(sum_tiles(turned[source].astype(jnp.float32) * receiver_row))
            same = gather_rows(same)
            crossed = gather_rows(crossed)
            lane = lax.broadcasted_iota(jnp.int32, same.shape, 1)
            rows = jnp.where(
                lane < half,
                same + pltpu.roll(same, half, 1),
                pltpu.roll(crossed, half, 1) - crossed,
            )
            place = pl.ds(pl.multiple_of(first + offset, 8), 8)
            if add:
                rows = rows + total[place, :]
            total[place, :] = rows
        return carry

    lax.fori_loop(0, count // GROUP, step, 0)


def turn_rows(near, turned):
    half = turned.shape[2] // 2

    def step(channel, carry):
        turned[channel] = pltpu.roll(near[channel].astype(jnp.float32), half, 1).astype(
            jnp.bfloat16
        )
        return carry

    lax.fori_loop(0, turned.shape[0], step, 0, unroll=8)


def exchange_kernel(
    nchan, ntm, sources, receivers, owners, tapering, own, total, slots, *scratch
):
    chunks = own.shape[1] // CHUNK
    near = scratch[:chunks]
    (
        turned, mine, from_left, to_right, from_right, to_left,
        own_sems, far_send, far_recv, pass_send, pass_recv,
        right_send, right_recv, left_send, left_recv,
    ) = scratch[chunks:]
    rows = own.shape[0]
    piece_rows = rows // PIECES
    chan = lax.axis_index("chan")
    me = lax.axis_index("tm")
    core = lax.rem(chan, 2)
    partner = chan + 1 - 2 * core
    behind = lax.rem(chan + nchan - 2, nchan)
    beyond = lax.rem(chan + 2, nchan)
    last = ntm - 1

    barrier = pltpu.get_barrier_semaphore()
    peers = (behind, partner) if nchan == 4 else (behind, beyond, partner)
    for device in peers:
        pl.semaphore_signal(barrier, inc=1, device_id={"chan": device}, device_id_type=MESH)

    @pl.when(me > 0)
    def _():
        pl.semaphore_signal(barrier, inc=1, device_id={"tm": me - 1}, device_id_type=MESH)

    @pl.when(me < last)
    def _():
        pl.semaphore_signal(barrier, inc=1, device_id={"tm": me + 1}, device_id_type=MESH)

    own_copies = []
    for chunk in range(chunks):
        copy = pltpu.make_async_copy(
            own.at[:, pl.ds(chunk * CHUNK, CHUNK), :],
            near[chunk].at[pl.ds(0, rows)],
            own_sems.at[chunk],
        )
        own_copies.append(copy)
    own_copies[0].start()

    pl.semaphore_wait(
        barrier, len(peers) + (me > 0).astype(jnp.int32) + (me < last).astype(jnp.int32)
    )

    def own_piece(number):
        chunk, piece = divmod(number, PIECES)
        return own.at[pl.ds(piece * piece_rows, piece_rows), pl.ds(chunk * CHUNK, CHUNK), :]

    def near_piece(number, block):
        chunk, piece = divmod(number, PIECES)
        return near[chunk].at[pl.ds(block * rows + piece * piece_rows, piece_rows)]

    def far(number):
        return pltpu.make_async_remote_copy(
            src_ref=own_piece(number),
            dst_ref=near_piece(number, 2),
            send_sem=far_send.at[number],
            recv_sem=far_recv.at[number],
            device_id={"chan": behind},
            device_id_type=MESH,
        )

    def handed(number, source):
        return pltpu.make_async_remote_copy(
            src_ref=source,
            dst_ref=near_piece(number, 1),
            send_sem=pass_send.at[number],
            recv_sem=pass_recv.at[number],
            device_id={"chan": partner},
            device_id_type=MESH,
        )

    count = chunks * PIECES
    for number in range(min(DEPTH, count)):
        far(number).start()

    for copy in own_copies[1:]:
        copy.start()

    @pl.when(core == 1)
    def _():
        for number in range(count):
            handed(number, own_piece(number)).start()

    def arrive(number):
        far(number).wait_recv()
        if number + DEPTH < count:
            far(number + DEPTH).start()

        @pl.when(core == 0)
        def _():
            handed(number, near_piece(number, 2)).start()

    group_rows = mine.shape[0] // FLOWS

    def count_slots(group, held):
        for k in range(16):
            pair = group * 16 + k
            slots[pair] = held
            held = held + (owners[pair] == me).astype(jnp.int32)
        return held

    for chunk in range(chunks):
        own_copies[chunk].wait()
        turn_rows(near[chunk], turned)
        if chunk == 0:
            slots[mine.shape[0]] = lax.fori_loop(
                0, mine.shape[0] // 16, count_slots, jnp.int32(0)
            )
        for piece in range(PIECES):
            arrive(chunk * PIECES + piece)
        for piece in range(PIECES):
            handed(chunk * PIECES + piece, own_piece(chunk * PIECES + piece)).wait_recv()
        if chunk < chunks - 1:
            cross_rows(
                sources, receivers, near[chunk], turned, mine, 0, mine.shape[0], chunk > 0
            )

    def flow(source, target, send_sem, recv_sem, group, device):
        place = pl.ds(pl.multiple_of(group * group_rows, group_rows), group_rows)
        return pltpu.make_async_remote_copy(
            src_ref=source.at[place],
            dst_ref=target.at[place],
            send_sem=send_sem.at[group],
            recv_sem=recv_sem.at[group],
            device_id={"tm": device},
            device_id_type=MESH,
        )

    def rightward(group):
        return flow(to_right, from_left, right_send, right_recv, group, lax.rem(me + 1, ntm))

    def leftward(group):
        return flow(to_left, from_right, left_send, left_recv, group, lax.rem(me + last, ntm))

    def place_of(group):
        return pl.ds(pl.multiple_of(group * group_rows, group_rows), group_rows)

    def stage(step, carry):
        @pl.when(step < FLOWS)
        def _():
            cross_rows(
                sources, receivers, near[chunks - 1], turned, mine,
                step * group_rows, group_rows, chunks > 1,
            )

        right_group = step - LAG * me

        @pl.when((right_group >= 0) & (right_group < FLOWS) & (me < last))
        def _():
            place = place_of(right_group)

            @pl.when(me > 0)
            def _():
                rightward(right_group).wait_recv()
                to_right[place, :] = mine[place, :] + from_left[place, :]

            @pl.when(me == 0)
            def _():
                to_right[place, :] = mine[place, :]

            rightward(right_group).start()

        left_group = step - LAG * (last - me)

        @pl.when((left_group >= 0) & (left_group < FLOWS) & (me > 0))
        def _():
            place = place_of(left_group)

            @pl.when(me < last)
            def _():
                leftward(left_group).wait_recv()
                to_left[place, :] = mine[place, :] + from_right[place, :]

            @pl.when(me == last)
            def _():
                to_left[place, :] = mine[place, :]

            leftward(left_group).start()

        return carry

    lax.fori_loop(0, FLOWS + LAG * last, stage, 0)

    def finish(group, carry):
        place = place_of(group)
        taper = jnp.transpose(
            jnp.broadcast_to(tapering[pl.ds(group, 1), :], (total.shape[1], group_rows))
        )

        @pl.when(me == 0)
        def _():
            leftward(group).wait_recv()
            total[place, :] = (mine[place, :] + from_right[place, :]) * taper

        @pl.when(me == last)
        def _():
            rightward(group).wait_recv()
            total[place, :] = (mine[place, :] + from_left[place, :]) * taper

        @pl.when((me > 0) & (me < last))
        def _():
            total[place, :] = (to_right[place, :] + from_right[place, :]) * taper

        @pl.when(me < last)
        def _():
            rightward(group).wait_send()

        @pl.when(me > 0)
        def _():
            leftward(group).wait_send()

        return carry

    lax.fori_loop(0, FLOWS, finish, 0)
    for number in range(count):
        far(number).wait_send()
        handed(number, own_piece(number)).wait_send()


def stack_kernel(slots, sums, table, out, rows):
    npairs = sums.shape[0]
    capacity, length = out.shape
    rows[...] = jnp.zeros_like(rows)

    def step(group, carry):
        first = pl.multiple_of(group * 32, 32)
        for k in range(0, 32, 8):
            tile = sums[pl.ds(pl.multiple_of(first + k, 8), 8), :]
            for j in range(8):
                rows[pl.ds(slots[first + k + j], 1), :] = tile[j : j + 1]
        return carry

    lax.fori_loop(0, npairs // 32, step, 0)
    rows[pl.ds(slots[npairs], 1), :] = jnp.zeros((1, length), jnp.float32)
    out[...] = jnp.dot(
        rows[0:capacity, :],
        table[...],
        precision=lax.Precision.HIGHEST,
        preferred_element_type=jnp.float32,
    )


def shards(spectra, band_width, pair_list, owner_ids):
    channel_rows, window_rows, length = spectra.shape
    npairs = pair_list.shape[1]
    tm_size = lax.axis_size("tm")
    capacity = 2 * npairs // tm_size
    windows = window_rows * tm_size
    sources = pair_list[0]
    offsets = pair_list[1]
    receivers = sources + offsets
    smem = pl.BlockSpec(memory_space=pltpu.SMEM)
    vmem = pl.BlockSpec(memory_space=pltpu.VMEM)
    hbm = pl.BlockSpec(memory_space=pl.ANY)
    tapering = (1.0 - offsets.astype(jnp.float32) / band_width[0].astype(jnp.float32)) / windows
    tapering = tapering.reshape(FLOWS, npairs // FLOWS)
    chunks = window_rows // CHUNK
    flow_buffer = pltpu.VMEM((npairs, length), jnp.float32)
    total, slots = pl.pallas_call(
        functools.partial(exchange_kernel, lax.axis_size("chan"), tm_size),
        out_shape=(
            jax.ShapeDtypeStruct((npairs, length), jnp.float32),
            jax.ShapeDtypeStruct((npairs + 1,), jnp.int32),
        ),
        in_specs=[smem, smem, smem, vmem, hbm],
        out_specs=(vmem, smem),
        scratch_shapes=[pltpu.VMEM(((K_SH + 1) * channel_rows, CHUNK, length), jnp.bfloat16)] * chunks
        + [pltpu.VMEM((channel_rows, CHUNK, length), jnp.bfloat16)]
        + [flow_buffer] * 5
        + [pltpu.SemaphoreType.DMA((chunks,))]
        + [pltpu.SemaphoreType.DMA((chunks * PIECES,))] * 4
        + [pltpu.SemaphoreType.DMA((FLOWS,))] * 4,
        compiler_params=pltpu.CompilerParams(
            vmem_limit_bytes=48 * 2**20, collective_id=0, has_side_effects=True
        ),
        cost_estimate=pl.CostEstimate(
            flops=8 * npairs * window_rows * length, bytes_accessed=14 * 2**20, transcendentals=0
        ),
    )(sources, receivers, owner_ids, tapering, spectra)
    return pl.pallas_call(
        stack_kernel,
        out_shape=jax.ShapeDtypeStruct((capacity, length), jnp.float32),
        in_specs=[smem, vmem, vmem],
        out_specs=vmem,
        scratch_shapes=[pltpu.VMEM((capacity + 8, length), jnp.float32)],
        compiler_params=pltpu.CompilerParams(vmem_limit_bytes=32 * 2**20),
        cost_estimate=pl.CostEstimate(
            flops=12 * capacity * length * length, bytes_accessed=3 * 2**20, transcendentals=0
        ),
    )(slots, total, jnp.asarray(inverse_table(length // 2)))


def solution(mesh):
    return jax.shard_map(
        shards,
        mesh=mesh,
        in_specs=(
            P(("grp", "chan"), "tm", None),
            P(("grp", "chan")),
            P(None, ("grp", "chan")),
            P(("grp", "chan")),
        ),
        out_specs=P(("grp", "chan", "tm"), None),
        check_vma=False,
    )
```

```python
import functools
import math

import jax
import jax.numpy as jnp
import numpy as np
from jax import lax
from jax.experimental import pallas as pl
from jax.experimental.pallas import tpu as pltpu
from jax.sharding import PartitionSpec as P

K_SH = 2
GROUP = 16
CHUNK = 16
PIECES = 8
DEPTH = 8
FLOWS = 32
LAG = 2
MESH = pl.DeviceIdType.MESH


def inverse_table(half_bins):
    length = 2 * half_bins
    row_ids = np.arange(length)
    frequency = row_ids % half_bins
    phases = (frequency[:, None] * np.arange(length)[None, :] % length) * (2.0 * math.pi / length)
    weights = np.where(frequency == 0, 1.0, 2.0)[:, None]
    return np.where(
        (row_ids >= half_bins)[:, None], -weights * np.sin(phases), weights * np.cos(phases)
    ).astype(np.float32)


def gather_rows(parts):
    row = lax.broadcasted_iota(jnp.int32, parts[0].shape, 0)
    span = 4
    while span:
        keep = (row // span) % 2 == 0
        half = len(parts) // 2
        parts = [
            jnp.where(keep, parts[k], pltpu.roll(parts[k + half], span, 0))
            + jnp.where(keep, pltpu.roll(parts[k], 8 - span, 0), parts[k + half])
            for k in range(half)
        ]
        span //= 2
    return parts[0]


def sum_tiles(rows):
    total = rows[0:8]
    for start in range(8, rows.shape[0], 8):
        total = total + rows[start : start + 8]
    return total


def cross_rows(sources, receivers, near, turned, total, start, count, add):
    half = total.shape[1] // 2

    def step(group, carry):
        first = pl.multiple_of(start + group * GROUP, GROUP)
        for offset in range(0, GROUP, 8):
            same, crossed = [], []
            for k in range(8):
                pair = first + offset + k
                source = sources[pair]
                receiver_row = near[receivers[pair]].astype(jnp.float32)
                same.append(sum_tiles(near[source].astype(jnp.float32) * receiver_row))
                crossed.append(sum_tiles(turned[source].astype(jnp.float32) * receiver_row))
            same = gather_rows(same)
            crossed = gather_rows(crossed)
            lane = lax.broadcasted_iota(jnp.int32, same.shape, 1)
            rows = jnp.where(
                lane < half,
                same + pltpu.roll(same, half, 1),
                pltpu.roll(crossed, half, 1) - crossed,
            )
            place = pl.ds(pl.multiple_of(first + offset, 8), 8)
            if add:
                rows = rows + total[place, :]
            total[place, :] = rows
        return carry

    lax.fori_loop(0, count // GROUP, step, 0)


def turn_rows(near, turned):
    half = turned.shape[2] // 2

    def step(channel, carry):
        turned[channel] = pltpu.roll(near[channel].astype(jnp.float32), half, 1).astype(
            jnp.bfloat16
        )
        return carry

    lax.fori_loop(0, turned.shape[0], step, 0, unroll=8)


def exchange_kernel(
    nchan, ntm, sources, receivers, owners, tapering, own, total, slots, *scratch
):
    chunks = own.shape[1] // CHUNK
    near = scratch[:chunks]
    (
        turned, mine, from_left, to_right, from_right, to_left,
        own_sems, far_send, far_recv, pass_send, pass_recv,
        right_send, right_recv, left_send, left_recv,
    ) = scratch[chunks:]
    rows = own.shape[0]
    piece_rows = rows // PIECES
    chan = lax.axis_index("chan")
    me = lax.axis_index("tm")
    core = lax.rem(chan, 2)
    partner = chan + 1 - 2 * core
    behind = lax.rem(chan + nchan - 2, nchan)
    beyond = lax.rem(chan + 2, nchan)
    last = ntm - 1

    barrier = pltpu.get_barrier_semaphore()
    peers = (behind, partner) if nchan == 4 else (behind, beyond, partner)
    for device in peers:
        pl.semaphore_signal(barrier, inc=1, device_id={"chan": device}, device_id_type=MESH)

    @pl.when(me > 0)
    def _():
        pl.semaphore_signal(barrier, inc=1, device_id={"tm": me - 1}, device_id_type=MESH)

    @pl.when(me < last)
    def _():
        pl.semaphore_signal(barrier, inc=1, device_id={"tm": me + 1}, device_id_type=MESH)

    own_copies = []
    for chunk in range(chunks):
        copy = pltpu.make_async_copy(
            own.at[:, pl.ds(chunk * CHUNK, CHUNK), :],
            near[chunk].at[pl.ds(0, rows)],
            own_sems.at[chunk],
        )
        own_copies.append(copy)
    own_copies[0].start()

    pl.semaphore_wait(
        barrier, len(peers) + (me > 0).astype(jnp.int32) + (me < last).astype(jnp.int32)
    )

    def own_piece(number):
        chunk, piece = divmod(number, PIECES)
        return own.at[pl.ds(piece * piece_rows, piece_rows), pl.ds(chunk * CHUNK, CHUNK), :]

    def near_piece(number, block):
        chunk, piece = divmod(number, PIECES)
        return near[chunk].at[pl.ds(block * rows + piece * piece_rows, piece_rows)]

    def far(number):
        return pltpu.make_async_remote_copy(
            src_ref=own_piece(number),
            dst_ref=near_piece(number, 2),
            send_sem=far_send.at[number],
            recv_sem=far_recv.at[number],
            device_id={"chan": behind},
            device_id_type=MESH,
        )

    def handed(number, source):
        return pltpu.make_async_remote_copy(
            src_ref=source,
            dst_ref=near_piece(number, 1),
            send_sem=pass_send.at[number],
            recv_sem=pass_recv.at[number],
            device_id={"chan": partner},
            device_id_type=MESH,
        )

    count = chunks * PIECES
    for number in range(min(DEPTH, count)):
        far(number).start()

    for copy in own_copies[1:]:
        copy.start()

    @pl.when(core == 1)
    def _():
        for number in range(count):
            handed(number, own_piece(number)).start()

    def arrive(number):
        far(number).wait_recv()
        if number + DEPTH < count:
            far(number + DEPTH).start()

        @pl.when(core == 0)
        def _():
            handed(number, near_piece(number, 2)).start()

    group_rows = mine.shape[0] // FLOWS

    def count_slots(group, held):
        for k in range(16):
            pair = group * 16 + k
            slots[pair] = held
            held = held + (owners[pair] == me).astype(jnp.int32)
        return held

    for chunk in range(chunks):
        own_copies[chunk].wait()
        turn_rows(near[chunk], turned)
        if chunk == 0:
            slots[mine.shape[0]] = lax.fori_loop(
                0, mine.shape[0] // 16, count_slots, jnp.int32(0)
            )
        for piece in range(PIECES):
            arrive(chunk * PIECES + piece)
        for piece in range(PIECES):
            handed(chunk * PIECES + piece, own_piece(chunk * PIECES + piece)).wait_recv()
        if chunk < chunks - 1:
            cross_rows(
                sources, receivers, near[chunk], turned, mine, 0, mine.shape[0], chunk > 0
            )

    def flow(source, target, send_sem, recv_sem, group, device):
        place = pl.ds(pl.multiple_of(group * group_rows, group_rows), group_rows)
        return pltpu.make_async_remote_copy(
            src_ref=source.at[place],
            dst_ref=target.at[place],
            send_sem=send_sem.at[group],
            recv_sem=recv_sem.at[group],
            device_id={"tm": device},
            device_id_type=MESH,
        )

    def rightward(group):
        return flow(to_right, from_left, right_send, right_recv, group, lax.rem(me + 1, ntm))

    def leftward(group):
        return flow(to_left, from_right, left_send, left_recv, group, lax.rem(me + last, ntm))

    def place_of(group):
        return pl.ds(pl.multiple_of(group * group_rows, group_rows), group_rows)

    def finish(group):
        place = place_of(group)
        taper = jnp.transpose(
            jnp.broadcast_to(tapering[pl.ds(group, 1), :], (total.shape[1], group_rows))
        )

        @pl.when(me == 0)
        def _():
            leftward(group).wait_recv()
            total[place, :] = (mine[place, :] + from_right[place, :]) * taper

        @pl.when(me == last)
        def _():
            rightward(group).wait_recv()
            total[place, :] = (mine[place, :] + from_left[place, :]) * taper

        @pl.when((me > 0) & (me < last))
        def _():
            total[place, :] = (to_right[place, :] + from_right[place, :]) * taper

    def stage(step, carry):
        @pl.when(step < FLOWS)
        def _():
            cross_rows(
                sources, receivers, near[chunks - 1], turned, mine,
                step * group_rows, group_rows, chunks > 1,
            )

        right_group = step - LAG * me

        @pl.when((right_group >= 0) & (right_group < FLOWS) & (me < last))
        def _():
            place = place_of(right_group)

            @pl.when(me > 0)
            def _():
                rightward(right_group).wait_recv()
                to_right[place, :] = mine[place, :] + from_left[place, :]

            @pl.when(me == 0)
            def _():
                to_right[place, :] = mine[place, :]

            rightward(right_group).start()

        left_group = step - LAG * (last - me)

        @pl.when((left_group >= 0) & (left_group < FLOWS) & (me > 0))
        def _():
            place = place_of(left_group)

            @pl.when(me < last)
            def _():
                leftward(left_group).wait_recv()
                to_left[place, :] = mine[place, :] + from_right[place, :]

            @pl.when(me == last)
            def _():
                to_left[place, :] = mine[place, :]

            leftward(left_group).start()

        whole_group = step - LAG * last

        @pl.when(whole_group >= 0)
        def _():
            finish(whole_group)

        return carry

    lax.fori_loop(0, FLOWS + LAG * last, stage, 0)

    def settle(group, carry):
        @pl.when(me < last)
        def _():
            rightward(group).wait_send()

        @pl.when(me > 0)
        def _():
            leftward(group).wait_send()

        return carry

    lax.fori_loop(0, FLOWS, settle, 0)
    for number in range(count):
        far(number).wait_send()
        handed(number, own_piece(number)).wait_send()


def stack_kernel(slots, sums, table, out, rows):
    npairs = sums.shape[0]
    capacity, length = out.shape
    rows[...] = jnp.zeros_like(rows)

    def step(group, carry):
        first = pl.multiple_of(group * 32, 32)
        for k in range(0, 32, 8):
            tile = sums[pl.ds(pl.multiple_of(first + k, 8), 8), :]
            for j in range(8):
                rows[pl.ds(slots[first + k + j], 1), :] = tile[j : j + 1]
        return carry

    lax.fori_loop(0, npairs // 32, step, 0)
    rows[pl.ds(slots[npairs], 1), :] = jnp.zeros((1, length), jnp.float32)
    out[...] = jnp.dot(
        rows[0:capacity, :],
        table[...],
        precision=lax.Precision.HIGHEST,
        preferred_element_type=jnp.float32,
    )


def shards(spectra, band_width, pair_list, owner_ids):
    channel_rows, window_rows, length = spectra.shape
    npairs = pair_list.shape[1]
    tm_size = lax.axis_size("tm")
    capacity = 2 * npairs // tm_size
    windows = window_rows * tm_size
    sources = pair_list[0]
    offsets = pair_list[1]
    receivers = sources + offsets
    smem = pl.BlockSpec(memory_space=pltpu.SMEM)
    vmem = pl.BlockSpec(memory_space=pltpu.VMEM)
    hbm = pl.BlockSpec(memory_space=pl.ANY)
    tapering = (1.0 - offsets.astype(jnp.float32) / band_width[0].astype(jnp.float32)) / windows
    tapering = tapering.reshape(FLOWS, npairs // FLOWS)
    chunks = window_rows // CHUNK
    flow_buffer = pltpu.VMEM((npairs, length), jnp.float32)
    total, slots = pl.pallas_call(
        functools.partial(exchange_kernel, lax.axis_size("chan"), tm_size),
        out_shape=(
            jax.ShapeDtypeStruct((npairs, length), jnp.float32),
            jax.ShapeDtypeStruct((npairs + 1,), jnp.int32),
        ),
        in_specs=[smem, smem, smem, vmem, hbm],
        out_specs=(vmem, smem),
        scratch_shapes=[pltpu.VMEM(((K_SH + 1) * channel_rows, CHUNK, length), jnp.bfloat16)] * chunks
        + [pltpu.VMEM((channel_rows, CHUNK, length), jnp.bfloat16)]
        + [flow_buffer] * 5
        + [pltpu.SemaphoreType.DMA((chunks,))]
        + [pltpu.SemaphoreType.DMA((chunks * PIECES,))] * 4
        + [pltpu.SemaphoreType.DMA((FLOWS,))] * 4,
        compiler_params=pltpu.CompilerParams(
            vmem_limit_bytes=48 * 2**20, collective_id=0, has_side_effects=True
        ),
        cost_estimate=pl.CostEstimate(
            flops=8 * npairs * window_rows * length, bytes_accessed=14 * 2**20, transcendentals=0
        ),
    )(sources, receivers, owner_ids, tapering, spectra)
    return pl.pallas_call(
        stack_kernel,
        out_shape=jax.ShapeDtypeStruct((capacity, length), jnp.float32),
        in_specs=[smem, vmem, vmem],
        out_specs=vmem,
        scratch_shapes=[pltpu.VMEM((capacity + 8, length), jnp.float32)],
        compiler_params=pltpu.CompilerParams(vmem_limit_bytes=32 * 2**20),
        cost_estimate=pl.CostEstimate(
            flops=12 * capacity * length * length, bytes_accessed=3 * 2**20, transcendentals=0
        ),
    )(slots, total, jnp.asarray(inverse_table(length // 2)))


def solution(mesh):
    return jax.shard_map(
        shards,
        mesh=mesh,
        in_specs=(
            P(("grp", "chan"), "tm", None),
            P(("grp", "chan")),
            P(None, ("grp", "chan")),
            P(("grp", "chan")),
        ),
        out_specs=P(("grp", "chan", "tm"), None),
        check_vma=False,
    )
```

```python
import functools
import math

import jax
import jax.numpy as jnp
import numpy as np
from jax import lax
from jax.experimental import pallas as pl
from jax.experimental.pallas import tpu as pltpu
from jax.sharding import PartitionSpec as P

K_SH = 2
GROUP = 16
CHUNK = 16
PIECES = 8
DEPTH = 8
FLOWS = 32
LAG = 4
MESH = pl.DeviceIdType.MESH


def inverse_table(half_bins):
    length = 2 * half_bins
    row_ids = np.arange(length)
    frequency = row_ids % half_bins
    phases = (frequency[:, None] * np.arange(length)[None, :] % length) * (2.0 * math.pi / length)
    weights = np.where(frequency == 0, 1.0, 2.0)[:, None]
    return np.where(
        (row_ids >= half_bins)[:, None], -weights * np.sin(phases), weights * np.cos(phases)
    ).astype(np.float32)


def gather_rows(parts):
    row = lax.broadcasted_iota(jnp.int32, parts[0].shape, 0)
    span = 4
    while span:
        keep = (row // span) % 2 == 0
        half = len(parts) // 2
        parts = [
            jnp.where(keep, parts[k], pltpu.roll(parts[k + half], span, 0))
            + jnp.where(keep, pltpu.roll(parts[k], 8 - span, 0), parts[k + half])
            for k in range(half)
        ]
        span //= 2
    return parts[0]


def sum_tiles(rows):
    total = rows[0:8]
    for start in range(8, rows.shape[0], 8):
        total = total + rows[start : start + 8]
    return total


def cross_rows(sources, receivers, near, turned, total, start, count, add):
    half = total.shape[1] // 2

    def step(group, carry):
        first = pl.multiple_of(start + group * GROUP, GROUP)
        for offset in range(0, GROUP, 8):
            same, crossed = [], []
            for k in range(8):
                pair = first + offset + k
                source = sources[pair]
                receiver_row = near[receivers[pair]].astype(jnp.float32)
                same.append(sum_tiles(near[source].astype(jnp.float32) * receiver_row))
                crossed.append(sum_tiles(turned[source].astype(jnp.float32) * receiver_row))
            same = gather_rows(same)
            crossed = gather_rows(crossed)
            lane = lax.broadcasted_iota(jnp.int32, same.shape, 1)
            rows = jnp.where(
                lane < half,
                same + pltpu.roll(same, half, 1),
                pltpu.roll(crossed, half, 1) - crossed,
            )
            place = pl.ds(pl.multiple_of(first + offset, 8), 8)
            if add:
                rows = rows + total[place, :]
            total[place, :] = rows
        return carry

    lax.fori_loop(0, count // GROUP, step, 0)


def turn_rows(near, turned):
    half = turned.shape[2] // 2

    def step(channel, carry):
        turned[channel] = pltpu.roll(near[channel].astype(jnp.float32), half, 1).astype(
            jnp.bfloat16
        )
        return carry

    lax.fori_loop(0, turned.shape[0], step, 0, unroll=8)


def exchange_kernel(
    nchan, ntm, sources, receivers, owners, tapering, own, total, slots, *scratch
):
    chunks = own.shape[1] // CHUNK
    near = scratch[:chunks]
    (
        turned, mine, from_left, to_right, from_right, to_left,
        own_sems, far_send, far_recv, pass_send, pass_recv,
        right_send, right_recv, left_send, left_recv,
    ) = scratch[chunks:]
    rows = own.shape[0]
    piece_rows = rows // PIECES
    chan = lax.axis_index("chan")
    me = lax.axis_index("tm")
    core = lax.rem(chan, 2)
    partner = chan + 1 - 2 * core
    behind = lax.rem(chan + nchan - 2, nchan)
    beyond = lax.rem(chan + 2, nchan)
    last = ntm - 1

    barrier = pltpu.get_barrier_semaphore()
    peers = (behind, partner) if nchan == 4 else (behind, beyond, partner)
    for device in peers:
        pl.semaphore_signal(barrier, inc=1, device_id={"chan": device}, device_id_type=MESH)

    @pl.when(me > 0)
    def _():
        pl.semaphore_signal(barrier, inc=1, device_id={"tm": me - 1}, device_id_type=MESH)

    @pl.when(me < last)
    def _():
        pl.semaphore_signal(barrier, inc=1, device_id={"tm": me + 1}, device_id_type=MESH)

    own_copies = []
    for chunk in range(chunks):
        copy = pltpu.make_async_copy(
            own.at[:, pl.ds(chunk * CHUNK, CHUNK), :],
            near[chunk].at[pl.ds(0, rows)],
            own_sems.at[chunk],
        )
        own_copies.append(copy)
    own_copies[0].start()

    pl.semaphore_wait(
        barrier, len(peers) + (me > 0).astype(jnp.int32) + (me < last).astype(jnp.int32)
    )

    def own_piece(number):
        chunk, piece = divmod(number, PIECES)
        return own.at[pl.ds(piece * piece_rows, piece_rows), pl.ds(chunk * CHUNK, CHUNK), :]

    def near_piece(number, block):
        chunk, piece = divmod(number, PIECES)
        return near[chunk].at[pl.ds(block * rows + piece * piece_rows, piece_rows)]

    def far(number):
        return pltpu.make_async_remote_copy(
            src_ref=own_piece(number),
            dst_ref=near_piece(number, 2),
            send_sem=far_send.at[number],
            recv_sem=far_recv.at[number],
            device_id={"chan": behind},
            device_id_type=MESH,
        )

    def handed(number, source):
        return pltpu.make_async_remote_copy(
            src_ref=source,
            dst_ref=near_piece(number, 1),
            send_sem=pass_send.at[number],
            recv_sem=pass_recv.at[number],
            device_id={"chan": partner},
            device_id_type=MESH,
        )

    count = chunks * PIECES
    for number in range(min(DEPTH, count)):
        far(number).start()

    for copy in own_copies[1:]:
        copy.start()

    @pl.when(core == 1)
    def _():
        for number in range(count):
            handed(number, own_piece(number)).start()

    def arrive(number):
        far(number).wait_recv()
        if number + DEPTH < count:
            far(number + DEPTH).start()

        @pl.when(core == 0)
        def _():
            handed(number, near_piece(number, 2)).start()

    group_rows = mine.shape[0] // FLOWS

    def count_slots(group, held):
        for k in range(16):
            pair = group * 16 + k
            slots[pair] = held
            held = held + (owners[pair] == me).astype(jnp.int32)
        return held

    for chunk in range(chunks):
        own_copies[chunk].wait()
        turn_rows(near[chunk], turned)
        if chunk == 0:
            slots[mine.shape[0]] = lax.fori_loop(
                0, mine.shape[0] // 16, count_slots, jnp.int32(0)
            )
        for piece in range(PIECES):
            arrive(chunk * PIECES + piece)
        for piece in range(PIECES):
            handed(chunk * PIECES + piece, own_piece(chunk * PIECES + piece)).wait_recv()
        if chunk < chunks - 1:
            cross_rows(
                sources, receivers, near[chunk], turned, mine, 0, mine.shape[0], chunk > 0
            )

    def flow(source, target, send_sem, recv_sem, group, device):
        place = pl.ds(pl.multiple_of(group * group_rows, group_rows), group_rows)
        return pltpu.make_async_remote_copy(
            src_ref=source.at[place],
            dst_ref=target.at[place],
            send_sem=send_sem.at[group],
            recv_sem=recv_sem.at[group],
            device_id={"tm": device},
            device_id_type=MESH,
        )

    def rightward(group):
        return flow(to_right, from_left, right_send, right_recv, group, lax.rem(me + 1, ntm))

    def leftward(group):
        return flow(to_left, from_right, left_send, left_recv, group, lax.rem(me + last, ntm))

    def place_of(group):
        return pl.ds(pl.multiple_of(group * group_rows, group_rows), group_rows)

    def stage(step, carry):
        @pl.when(step < FLOWS)
        def _():
            cross_rows(
                sources, receivers, near[chunks - 1], turned, mine,
                step * group_rows, group_rows, chunks > 1,
            )

        right_group = step - LAG * me

        @pl.when((right_group >= 0) & (right_group < FLOWS) & (me < last))
        def _():
            place = place_of(right_group)

            @pl.when(me > 0)
            def _():
                rightward(right_group).wait_recv()
                to_right[place, :] = mine[place, :] + from_left[place, :]

            @pl.when(me == 0)
            def _():
                to_right[place, :] = mine[place, :]

            rightward(right_group).start()

        left_group = step - LAG * (last - me)

        @pl.when((left_group >= 0) & (left_group < FLOWS) & (me > 0))
        def _():
            place = place_of(left_group)

            @pl.when(me < last)
            def _():
                leftward(left_group).wait_recv()
                to_left[place, :] = mine[place, :] + from_right[place, :]

            @pl.when(me == last)
            def _():
                to_left[place, :] = mine[place, :]

            leftward(left_group).start()

        return carry

    lax.fori_loop(0, FLOWS + LAG * last, stage, 0)

    def finish(group, carry):
        place = place_of(group)
        taper = jnp.transpose(
            jnp.broadcast_to(tapering[pl.ds(group, 1), :], (total.shape[1], group_rows))
        )

        @pl.when(me == 0)
        def _():
            leftward(group).wait_recv()
            total[place, :] = (mine[place, :] + from_right[place, :]) * taper

        @pl.when(me == last)
        def _():
            rightward(group).wait_recv()
            total[place, :] = (mine[place, :] + from_left[place, :]) * taper

        @pl.when((me > 0) & (me < last))
        def _():
            total[place, :] = (to_right[place, :] + from_right[place, :]) * taper

        @pl.when(me < last)
        def _():
            rightward(group).wait_send()

        @pl.when(me > 0)
        def _():
            leftward(group).wait_send()

        return carry

    lax.fori_loop(0, FLOWS, finish, 0)
    for number in range(count):
        far(number).wait_send()
        handed(number, own_piece(number)).wait_send()


def stack_kernel(slots, sums, table, out, rows):
    npairs = sums.shape[0]
    capacity, length = out.shape
    rows[...] = jnp.zeros_like(rows)

    def step(group, carry):
        first = pl.multiple_of(group * 32, 32)
        for k in range(0, 32, 8):
            tile = sums[pl.ds(pl.multiple_of(first + k, 8), 8), :]
            for j in range(8):
                rows[pl.ds(slots[first + k + j], 1), :] = tile[j : j + 1]
        return carry

    lax.fori_loop(0, npairs // 32, step, 0)
    rows[pl.ds(slots[npairs], 1), :] = jnp.zeros((1, length), jnp.float32)
    out[...] = jnp.dot(
        rows[0:capacity, :],
        table[...],
        precision=lax.Precision.HIGHEST,
        preferred_element_type=jnp.float32,
    )


def shards(spectra, band_width, pair_list, owner_ids):
    channel_rows, window_rows, length = spectra.shape
    npairs = pair_list.shape[1]
    tm_size = lax.axis_size("tm")
    capacity = 2 * npairs // tm_size
    windows = window_rows * tm_size
    sources = pair_list[0]
    offsets = pair_list[1]
    receivers = sources + offsets
    smem = pl.BlockSpec(memory_space=pltpu.SMEM)
    vmem = pl.BlockSpec(memory_space=pltpu.VMEM)
    hbm = pl.BlockSpec(memory_space=pl.ANY)
    tapering = (1.0 - offsets.astype(jnp.float32) / band_width[0].astype(jnp.float32)) / windows
    tapering = tapering.reshape(FLOWS, npairs // FLOWS)
    chunks = window_rows // CHUNK
    flow_buffer = pltpu.VMEM((npairs, length), jnp.float32)
    total, slots = pl.pallas_call(
        functools.partial(exchange_kernel, lax.axis_size("chan"), tm_size),
        out_shape=(
            jax.ShapeDtypeStruct((npairs, length), jnp.float32),
            jax.ShapeDtypeStruct((npairs + 1,), jnp.int32),
        ),
        in_specs=[smem, smem, smem, vmem, hbm],
        out_specs=(vmem, smem),
        scratch_shapes=[pltpu.VMEM(((K_SH + 1) * channel_rows, CHUNK, length), jnp.bfloat16)] * chunks
        + [pltpu.VMEM((channel_rows, CHUNK, length), jnp.bfloat16)]
        + [flow_buffer] * 5
        + [pltpu.SemaphoreType.DMA((chunks,))]
        + [pltpu.SemaphoreType.DMA((chunks * PIECES,))] * 4
        + [pltpu.SemaphoreType.DMA((FLOWS,))] * 4,
        compiler_params=pltpu.CompilerParams(
            vmem_limit_bytes=48 * 2**20, collective_id=0, has_side_effects=True
        ),
        cost_estimate=pl.CostEstimate(
            flops=8 * npairs * window_rows * length, bytes_accessed=14 * 2**20, transcendentals=0
        ),
    )(sources, receivers, owner_ids, tapering, spectra)
    return pl.pallas_call(
        stack_kernel,
        out_shape=jax.ShapeDtypeStruct((capacity, length), jnp.float32),
        in_specs=[smem, vmem, vmem],
        out_specs=vmem,
        scratch_shapes=[pltpu.VMEM((capacity + 8, length), jnp.float32)],
        compiler_params=pltpu.CompilerParams(vmem_limit_bytes=32 * 2**20),
        cost_estimate=pl.CostEstimate(
            flops=12 * capacity * length * length, bytes_accessed=3 * 2**20, transcendentals=0
        ),
    )(slots, total, jnp.asarray(inverse_table(length // 2)))


def solution(mesh):
    return jax.shard_map(
        shards,
        mesh=mesh,
        in_specs=(
            P(("grp", "chan"), "tm", None),
            P(("grp", "chan")),
            P(None, ("grp", "chan")),
            P(("grp", "chan")),
        ),
        out_specs=P(("grp", "chan", "tm"), None),
        check_vma=False,
    )
```
